32 devices in a mesh: groups: 2 (over y), fsdp: 4 (over z), dp: 2 (over x), sub: 2 (over core).
Axes of the slice: x: 2, y: 2, z: 4, core: 2. Of those that a mesh axis runs over, the one named last changes fastest.
Arguments:
- hidden: bfloat16 [32, 64, 28672], P(('groups', 'fsdp', 'dp'), None, 'sub'), parts along dimension 0, may hold values from -6 to 6
- out_grad: bfloat16 [32, 64, 8192], P(('groups', 'fsdp', 'dp'), None, 'sub'), parts along dimension 0, may hold values from -6 to 6
- proj_in: bfloat16 [2, 14336, 64], P('sub', 'fsdp'), may hold values from -0.03125 to 0.03125
- proj_out: bfloat16 [2, 4096, 64], P('sub', 'fsdp'), may hold values from -0.0625 to 0.0625
- queries: bfloat16 [1024, 4096], P('fsdp', 'sub'), may hold values from -6 to 6
- lengths: int32 [32], P(('groups', 'fsdp', 'dp')), parts along dimension 0, may hold values from 1 to 64, 768 in all
Outputs:
- covariance: float32 [8192, 4096], P(('groups', 'fsdp'), ('dp', 'sub')), parts along dimension 0
- scores: float32 [32, 1024], P(('groups', 'fsdp', 'dp')), parts along dimension 0
The draws below stay inside these ranges and needn't reach their ends.
There are 2 independent parts, one for each index of `groups`. The reference program is written for one: setup_inputs(seed, part) draws one part's arguments, and reference() takes and returns one part's arrays. A program takes and returns all parts, laid end to end along the dimension named above; an argument that names none is the same for every part. Nothing has to cross between parts.
Inputs may be any that keep to these rules, and one draw needn't show every extreme that they name: lengths[e] is the number of live token slots of example e; slots from lengths[e] on are padding; in each part along groups the lengths sum to 768, and some example of each part fills all 64 slots.
All inputs are finite; a program needn't handle non-finite values.
Results may differ from the reference program's by a relative error of at most 0.0041.
Values may be sent and summed in bfloat16 or wider, within the bound.
A program may use at most 128 MiB of HBM per device.

```python
import math
import jax
import jax.numpy as jnp
import numpy as np
from jax import lax

D = 8192
FF = 28672
K = 64
SLOT = 64
QUERIES = 1024
KK = 4096
EXAMPLES = 16
N_SUB = 2


def steps_of(own_key, shape, pieces, least, largest):
    gain = 1.0
    for dim, shards_of in pieces:
        draws = jax.random.uniform(jax.random.fold_in(jax.random.fold_in(own_key, 6), dim), (shards_of,), jnp.float32, least / len(pieces), largest / len(pieces))
        gain = gain * jnp.repeat(jnp.exp(draws), shape[dim] // shards_of).reshape((-1,) + (1,) * (len(shape) - 1 - dim))
    return gain


def profile(count, total, limit, skew):
    loads = [(1 << 20) // math.isqrt(grade ** skew) + 1 for grade in range(2, count + 1)]
    surplus, given = total - limit - (count - 1), [1] * (count - 1)
    while surplus > 0:
        movable = [i for i in range(count - 1) if given[i] < limit]
        pool, remaining = sum([loads[i] for i in movable]), surplus
        for i in movable:
            addition = min(limit - given[i], max(1, remaining * loads[i] // pool), surplus)
            given[i] = given[i] + addition
            surplus = surplus - addition
    return np.array([limit] + given)


def uneven(rng, count, total, limit, lean):
    if count == 2:
        one = jax.random.randint(rng, (), max(1, total - limit), min(limit, total - 1) + 1)
        return jnp.stack([one, total - one])
    sizes = jnp.asarray(profile(count, total, limit, lean), jnp.int32)
    twos = (count - 1) // 2
    giver, taker = sizes[1:1 + 2 * twos:2], sizes[2:2 + 2 * twos:2]
    room = jnp.minimum(giver - 1, limit - taker)
    moved = jax.random.randint(jax.random.fold_in(rng, 1), (twos,), 0, 1 << 20) % (room + 1)
    sizes = sizes.at[1:1 + 2 * twos:2].set(giver - moved).at[2:2 + 2 * twos:2].set(taker + moved)
    return sizes[jax.random.permutation(jax.random.fold_in(rng, 2), count)]


def gaussian(own_key, extent, deviation, limit, shards=(), kind=jnp.bfloat16):
    values = jax.random.normal(own_key, extent, jnp.float32) * deviation
    if len(shards) > 0:
        values = steps_of(own_key, extent, shards, -0.22, 0.18) * values
    return jnp.clip(values, min=-limit, max=limit).astype(kind)


def setup_inputs(seed: int = 0, part: int = 0) -> dict:
    seeds = jax.random.split(jax.random.key(seed), 7)
    part_splits = jax.random.split(jax.random.fold_in(seeds[6], part), 7)
    hidden = gaussian(part_splits[0], (EXAMPLES, SLOT, FF), 1.0, 6.0, ((0, 8), (2, 2)))
    out_grad = gaussian(part_splits[1], (EXAMPLES, SLOT, D), 1.0, 6.0, ((0, 8), (2, 2)))
    proj_in = gaussian(seeds[2], (N_SUB, FF // N_SUB, K), FF ** -0.5, 0.03125, ((0, 2), (1, 4)))
    proj_out = gaussian(seeds[3], (N_SUB, D // N_SUB, K), D ** -0.5, 0.0625, ((0, 2), (1, 4)))
    queries = gaussian(seeds[4], (QUERIES, KK), 1.0, 6.0, ((0, 4), (1, 2)))
    lengths = uneven(part_splits[5], EXAMPLES, EXAMPLES * SLOT * 3 // 4, SLOT, 0).astype(jnp.int32)
    return {"hidden": hidden, "out_grad": out_grad, "proj_in": proj_in, "proj_out": proj_out, "queries": queries, "lengths": lengths}


def reference(hidden, out_grad, proj_in, proj_out, queries, lengths):
    rows_in = hidden.reshape(EXAMPLES * SLOT, FF)
    rows_out = out_grad.reshape(EXAMPLES * SLOT, D)
    low_inputs = jnp.dot(rows_in, proj_in.reshape(FF, K), preferred_element_type=jnp.float32)
    low_grads = jnp.dot(rows_out, proj_out.reshape(D, K), preferred_element_type=jnp.float32)
    live_mask = (jnp.arange(SLOT, dtype=jnp.int32)[None, :] < lengths[:, None]).astype(jnp.float32)
    low_grads = low_grads.reshape(EXAMPLES, SLOT, K) * live_mask[:, :, None]
    low_inputs = low_inputs.reshape(EXAMPLES, SLOT, K)
    encoded = jnp.einsum('eta,etb->eab', low_grads, low_inputs, precision=lax.Precision.HIGHEST) / math.sqrt(SLOT)
    encoded = encoded.reshape(EXAMPLES, KK).astype(jnp.bfloat16)
    covariance = lax.dot_general(encoded, encoded, (((0,), (0,)), ((), ())), preferred_element_type=jnp.float32) / EXAMPLES
    scores = jnp.dot(encoded, queries.T, preferred_element_type=jnp.float32) / math.sqrt(KK)
    return (covariance, scores)
```

```python
import functools
import math

import jax
import jax.numpy as jnp
from jax import lax
from jax.experimental import pallas as pl
from jax.experimental.pallas import tpu as pltpu
from jax.sharding import PartitionSpec as P

MESH = pl.DeviceIdType.MESH
NT = (((1,), (1,)), ((), ()))


def kernel(F, hidden, out_grad, pin, pout, queries, lengths,
           rows_out, cols_out, scores_out,
           buf, hid, ogr, qry, acc, part, summed, gath, flat, enc, spart, sgot,
           local_sem, zs, xs, ys, dxs, dys, zr, xr, yr, dxr, dyr,
           sub_sem, es, er, ss, sr):
    g, f, d, s = (lax.axis_index(n) for n in ("groups", "fsdp", "dp", "sub"))
    W = pin.shape[0]
    kin, kout = pin.shape[1], pout.shape[1]
    L = kin + kout
    half = L // 2
    piece_rows = W // 4
    tokens = hidden.shape[0]
    E = enc.shape[0]

    loads = [
        pltpu.make_async_copy(pin, buf.at[f, :, pl.ds(0, kin)], local_sem.at[0]),
        pltpu.make_async_copy(pout, buf.at[f, :, pl.ds(kin, kout)], local_sem.at[1]),
    ]
    loads += [
        pltpu.make_async_copy(hidden.at[:, pl.ds(k * kin, kin)], hid.at[k], local_sem.at[3 + k])
        for k in range(F)
    ]
    loads += [
        pltpu.make_async_copy(out_grad.at[:, pl.ds(k * kout, kout)], ogr.at[k], local_sem.at[3 + F + k])
        for k in range(F)
    ]
    query_load = pltpu.make_async_copy(queries, qry, local_sem.at[2])
    for load in loads:
        load.start()
    query_load.start()

    barrier = pltpu.get_barrier_semaphore()
    others = [(df, dd, ds) for df in range(F) for dd in range(2) for ds in range(2)][1:]
    for df, dd, ds in others:
        pl.semaphore_signal(
            barrier, inc=1,
            device_id=(g, lax.rem(f + df, F), lax.rem(d + dd, 2), lax.rem(s + ds, 2)),
            device_id_type=MESH,
        )
    pl.semaphore_signal(barrier, inc=1, device_id=(1 - g, f, d, s), device_id_type=MESH)
    pl.semaphore_wait(barrier, len(others) + 1)

    mine = g * 2 + d
    col_x, col_y, col_d = g * 2 + (1 - d), (1 - g) * 2 + d, (1 - g) * 2 + (1 - d)
    dev_x, dev_y = (g, f, 1 - d, s), (1 - g, f, d, s)

    def piece(shard, col, lanes=None):
        rows = pl.ds(pl.multiple_of(col * piece_rows, piece_rows), piece_rows)
        if lanes is None:
            return buf.at[shard, rows, :]
        return buf.at[shard, rows, pl.ds(lanes * half, half)]

    def copy(ref, send, recv, dev):
        return pltpu.make_async_remote_copy(
            src_ref=ref, dst_ref=ref, send_sem=send, recv_sem=recv,
            device_id=dev, device_id_type=MESH,
        )

    def along_z(shard, up):
        dev = (g, f + 1, d, s) if up else (g, f - 1, d, s)
        return copy(piece(shard, mine), zs.at[1 if up else 0, shard], zr.at[shard], dev)

    def to_x(shard):
        return copy(piece(shard, mine), xs.at[shard], xr.at[shard], dev_x)

    def to_y(shard):
        return copy(piece(shard, mine), ys.at[shard], yr.at[shard], dev_y)

    def from_x(shard):
        return copy(piece(shard, col_x), xs.at[shard], xr.at[shard], dev_x)

    def from_y(shard):
        return copy(piece(shard, col_y), ys.at[shard], yr.at[shard], dev_y)

    def x_on_to_y(shard):
        return copy(piece(shard, col_x, 0), dys.at[shard], dyr.at[shard], dev_y)

    def y_on_to_x(shard):
        return copy(piece(shard, col_y, 1), dxs.at[shard], dxr.at[shard], dev_x)

    def diag_by_y(shard):
        return copy(piece(shard, col_d, 0), dys.at[shard], dyr.at[shard], dev_y)

    def diag_by_x(shard):
        return copy(piece(shard, col_d, 1), dxs.at[shard], dxr.at[shard], dev_x)

    def project(shard):
        acc[W:, :] += lax.dot_general(
            buf[shard, :, :kin], hid[shard], NT, preferred_element_type=jnp.float32)
        acc[:W, :] += lax.dot_general(
            buf[shard, :, kin:], ogr[shard], NT, preferred_element_type=jnp.float32)

    def each(t, fn):
        @pl.when(f - t >= 0)
        def _():
            fn(f - t, True)

        @pl.when(f + t < F)
        def _():
            fn(f + t, False)

    loads[0].wait()
    loads[1].wait()

    @pl.when(f > 0)
    def _():
        along_z(f, False).start()

    @pl.when(f < F - 1)
    def _():
        along_z(f, True).start()

    for load in loads[2:]:
        load.wait()
    acc[...] = jnp.zeros_like(acc)
    project(f)

    def arrive(shard, up):
        along_z(shard, up).wait_recv()
        if up:
            @pl.when(f < F - 1)
            def _():
                along_z(shard, True).start()
        else:
            @pl.when(f > 0)
            def _():
                along_z(shard, False).start()
        to_x(shard).start()
        to_y(shard).start()

    def relay(shard, up):
        from_x(shard).wait_recv()
        x_on_to_y(shard).start()
        from_y(shard).wait_recv()
        y_on_to_x(shard).start()

    def finish(shard, up):
        diag_by_y(shard).wait_recv()
        diag_by_x(shard).wait_recv()
        project(shard)

    for t in range(1, F + 2):
        if t < F:
            each(t, arrive)
        if 1 <= t - 1 < F:
            each(t - 1, relay)
        if 1 <= t - 2 < F:
            each(t - 2, finish)

    p_copy = pltpu.make_async_remote_copy(
        src_ref=acc, dst_ref=part, send_sem=sub_sem.at[0], recv_sem=sub_sem.at[1],
        device_id=(g, f, d, 1 - s), device_id_type=MESH,
    )
    p_copy.start()
    p_copy.wait_recv()
    summed[...] = acc[...] + part[...]

    slot = tokens // 2
    lane = lax.broadcasted_iota(jnp.int32, (W // 2, tokens), 1)
    even = summed[pl.ds(0, W // 2, stride=2), :]
    odd = summed[pl.ds(1, W // 2, stride=2), :]
    first = lane < lengths[0]
    second = jnp.logical_and(lane >= slot, lane < slot + lengths[1])
    left = jnp.concatenate(
        [jnp.where(first, even, 0.0), jnp.where(first, odd, 0.0),
         jnp.where(second, even, 0.0), jnp.where(second, odd, 0.0)], axis=0)
    outer = lax.dot_general(
        left, summed[W:, :], NT, precision=lax.Precision.HIGHEST,
        preferred_element_type=jnp.float32) / math.sqrt(slot)
    hw = W // 2
    pair = f * 2 + d
    own = pl.ds(pair * 2, 2)
    for i in range(2):
        both = jnp.concatenate(
            [outer[2 * i * hw:(2 * i + 1) * hw], outer[(2 * i + 1) * hw:(2 * i + 2) * hw]], axis=1)
        gath[pair * 2 + i] = both.astype(jnp.bfloat16)

    shifts = [(df, dd) for df in range(F) for dd in range(2)][1:]

    def enc_copy(k, owner, dev):
        ref = gath.at[pl.ds(owner * 2, 2)]
        return pltpu.make_async_remote_copy(
            src_ref=ref, dst_ref=ref, send_sem=es.at[k], recv_sem=er.at[owner],
            device_id=dev, device_id_type=MESH)

    def peer(df, dd):
        return lax.rem(f + df, F), lax.rem(d + dd, 2)

    for k, (df, dd) in enumerate(shifts):
        pf, pd = peer(df, dd)
        enc_copy(k, pair, (g, pf, pd, s)).start()
    query_load.wait()
    for k, (df, dd) in enumerate(shifts):
        pf, pd = peer(df, dd)
        enc_copy(k, pf * 2 + pd, (g, pf, pd, s)).wait_recv()

    for e in range(E):
        flat[e * hw:(e + 1) * hw, :] = gath[e].astype(jnp.float32)
    for r in range(hw):
        enc[:, r * 128:(r + 1) * 128] = flat[pl.ds(r, E, stride=hw), :].astype(jnp.bfloat16)

    dims = qry.shape[1]
    score = lax.dot_general(
        enc[:, pl.ds(pl.multiple_of(s * dims, dims), dims)], qry[...], NT,
        preferred_element_type=jnp.float32)
    for p in range(E // 2):
        spart[p] = score[2 * p:2 * p + 2, :]
    targets = [(df, ds) for df in range(F) for ds in range(2)]

    def score_copy(k, src, slot_id, dev):
        return pltpu.make_async_remote_copy(
            src_ref=spart.at[src], dst_ref=sgot.at[slot_id],
            send_sem=ss.at[k], recv_sem=sr.at[slot_id],
            device_id=dev, device_id_type=MESH)

    for k, (df, ds) in enumerate(targets[1:]):
        pf, ps = lax.rem(f + df, F), lax.rem(s + ds, 2)
        score_copy(k, pf * 2 + d, f * 2 + s, (g, pf, d, ps)).start()
    sgot[f * 2 + s] = spart[pair]
    nrow, ncol = rows_out.shape[1], cols_out.shape[1]
    rows_out[...] = enc[:, pl.ds(pl.multiple_of(f * nrow, nrow), nrow)]
    cols_out[...] = enc[:, pl.ds(pl.multiple_of((d * 2 + s) * ncol, ncol), ncol)]
    for k, (df, ds) in enumerate(targets[1:]):
        pf, ps = lax.rem(f + df, F), lax.rem(s + ds, 2)
        score_copy(k, pf * 2 + d, pf * 2 + ps, (g, pf, d, ps)).wait_recv()
    nq = qry.shape[0]
    for k in range(F):
        scores_out[:, k * nq:(k + 1) * nq] = (sgot[2 * k] + sgot[2 * k + 1]) / math.sqrt(2 * dims)

    for k, (df, ds) in enumerate(targets[1:]):
        pf, ps = lax.rem(f + df, F), lax.rem(s + ds, 2)
        score_copy(k, pf * 2 + d, f * 2 + s, (g, pf, d, ps)).wait_send()
    for k, (df, dd) in enumerate(shifts):
        pf, pd = peer(df, dd)
        enc_copy(k, pair, (g, pf, pd, s)).wait_send()
    p_copy.wait_send()

    @pl.when(f > 0)
    def _():
        along_z(f, False).wait_send()

    @pl.when(f < F - 1)
    def _():
        along_z(f, True).wait_send()

    def sent(shard, up):
        if up:
            @pl.when(f < F - 1)
            def _():
                along_z(shard, True).wait_send()
        else:
            @pl.when(f > 0)
            def _():
                along_z(shard, False).wait_send()
        to_x(shard).wait_send()
        to_y(shard).wait_send()
        x_on_to_y(shard).wait_send()
        y_on_to_x(shard).wait_send()

    for t in range(1, F):
        each(t, sent)


def fused(F, hidden, out_grad, proj_in, proj_out, queries, lengths):
    examples, slot_len, half_hidden = hidden.shape
    half_model = out_grad.shape[2]
    W = proj_in.shape[2]
    kin, kout = proj_in.shape[1], proj_out.shape[1]
    tokens = examples * slot_len
    nq, dims = queries.shape
    E = F * 2 * examples
    KK = W * W
    any_spec = pl.BlockSpec(memory_space=pl.ANY)
    vmem = pl.BlockSpec(memory_space=pltpu.VMEM)
    bf, f32 = jnp.bfloat16, jnp.float32
    dma = pltpu.SemaphoreType.DMA
    rows, cols, scores = pl.pallas_call(
        functools.partial(kernel, F),
        out_shape=(
            jax.ShapeDtypeStruct((E, KK // F), bf),
            jax.ShapeDtypeStruct((E, KK // 4), bf),
            jax.ShapeDtypeStruct((examples, nq * F), f32),
        ),
        in_specs=[any_spec] * 5 + [pl.BlockSpec(memory_space=pltpu.SMEM)],
        out_specs=(vmem, vmem, vmem),
        scratch_shapes=[
            pltpu.VMEM((F, W, kin + kout), bf),
            pltpu.VMEM((F, tokens, kin), bf),
            pltpu.VMEM((F, tokens, kout), bf),
            pltpu.VMEM((nq, dims), bf),
            pltpu.VMEM((2 * W, tokens), f32),
            pltpu.VMEM((2 * W, tokens), f32),
            pltpu.VMEM((2 * W, tokens), f32),
            pltpu.VMEM((E, W // 2, 2 * W), bf),
            pltpu.VMEM((E * W // 2, 2 * W), f32),
            pltpu.VMEM((E, KK), bf),
            pltpu.VMEM((E // 2, 2, nq), f32),
            pltpu.VMEM((2 * F, 2, nq), f32),
            dma((3 + 2 * F,)),
            dma((2, F)), dma((F,)), dma((F,)), dma((F,)), dma((F,)),
            dma((F,)), dma((F,)), dma((F,)), dma((F,)), dma((F,)),
            dma((2,)),
            dma((2 * F,)), dma((2 * F,)), dma((2 * F,)), dma((2 * F,)),
        ],
        compiler_params=pltpu.CompilerParams(
            collective_id=0, has_side_effects=True, vmem_limit_bytes=60 << 20),
    )(
        hidden.reshape(tokens, half_hidden),
        out_grad.reshape(tokens, half_model),
        jnp.swapaxes(proj_in[0], 0, 1),
        jnp.swapaxes(proj_out[0], 0, 1),
        queries,
        lengths,
    )
    covariance = lax.dot_general(
        rows, cols, (((0,), (0,)), ((), ())), preferred_element_type=f32) / E
    return covariance, scores


def general(hidden, out_grad, proj_in, proj_out, queries, lengths):
    examples, slot_len, half_hidden = hidden.shape
    half_model = out_grad.shape[2]
    W = proj_in.shape[2]
    tokens = examples * slot_len
    f32 = jnp.float32
    inputs_part = jnp.dot(
        hidden.reshape(tokens, half_hidden),
        lax.all_gather(proj_in, "fsdp", axis=1, tiled=True)[0],
        preferred_element_type=f32)
    grads_part = jnp.dot(
        out_grad.reshape(tokens, half_model),
        lax.all_gather(proj_out, "fsdp", axis=1, tiled=True)[0],
        preferred_element_type=f32)
    summed = lax.psum(jnp.concatenate((grads_part, inputs_part), axis=1), "sub")
    low_grads = summed[:, :W].reshape(examples, slot_len, W)
    low_inputs = summed[:, W:].reshape(examples, slot_len, W)
    live = (jnp.arange(slot_len, dtype=jnp.int32)[None, :] < lengths[:, None]).astype(f32)
    encoded = jnp.einsum(
        "eta,etb->eab", low_grads * live[:, :, None], low_inputs,
        precision=lax.Precision.HIGHEST) / math.sqrt(slot_len)
    KK = W * W
    encoded = encoded.reshape(examples, KK).astype(jnp.bfloat16)
    F, Dp, S = lax.axis_size("fsdp"), lax.axis_size("dp"), lax.axis_size("sub")
    everyone = lax.all_gather(encoded, ("fsdp", "dp"), axis=0, tiled=True)
    nrow, ncol, half = KK // F, KK // (Dp * S), KK // S
    rows = lax.dynamic_slice_in_dim(everyone, lax.axis_index("fsdp") * nrow, nrow, 1)
    cols = lax.dynamic_slice_in_dim(
        everyone, (lax.axis_index("dp") * S + lax.axis_index("sub")) * ncol, ncol, 1)
    covariance = lax.dot_general(
        rows, cols, (((0,), (0,)), ((), ())), preferred_element_type=f32) / everyone.shape[0]
    own_half = lax.dynamic_slice_in_dim(encoded, lax.axis_index("sub") * half, half, 1)
    partial_scores = lax.dot_general(
        own_half, lax.all_gather(queries, "fsdp", axis=0, tiled=True),
        (((1,), (1,)), ((), ())), preferred_element_type=f32)
    scores = lax.psum(partial_scores, "sub") / math.sqrt(KK)
    return covariance, scores


def solution(mesh):
    sizes = dict(mesh.shape)
    placed = (
        P(("groups", "fsdp", "dp"), None, "sub"),
        P(("groups", "fsdp", "dp"), None, "sub"),
        P("sub", "fsdp", None),
        P("sub", "fsdp", None),
        P("fsdp", "sub"),
        P(("groups", "fsdp", "dp")),
    )
    square = sizes["groups"] == 2 and sizes["dp"] == 2 and sizes["fsdp"] <= 4
    body = functools.partial(fused, sizes["fsdp"]) if square else general
    return jax.shard_map(
        body,
        mesh=mesh,
        in_specs=placed,
        out_specs=(P(("groups", "fsdp"), ("dp", "sub")), P(("groups", "fsdp", "dp"), None)),
        check_vma=False,
    )
```

```python
import functools
import math

import jax
import jax.numpy as jnp
from jax import lax
from jax.experimental import pallas as pl
from jax.experimental.pallas import tpu as pltpu
from jax.sharding import PartitionSpec as P

MESH = pl.DeviceIdType.MESH
NT = (((1,), (1,)), ((), ()))
PARTS = 3
THIRD = PARTS // 3
ITEMS = PARTS + THIRD
LAG = 3


def kernel(F, hidden, out_grad, pin, pout, queries, lengths,
           rows_out, cols_out, scores_out,
           buf, hid, ogr, qry, acc, part, summed, gath, flat, enc, spart, sgot,
           local_sem, zs, xs, ys, zr, xr, yr,
           sub_sem, es, er, ss, sr):
    g, f, d, s = (lax.axis_index(n) for n in ("groups", "fsdp", "dp", "sub"))
    W = pin.shape[0]
    kin, kout = pin.shape[1], pout.shape[1]
    L = kin + kout
    lanes = L // PARTS
    piece_rows = W // 4
    tokens = hidden.shape[0]
    E = enc.shape[0]

    loads = [
        pltpu.make_async_copy(pin, buf.at[f, :, pl.ds(0, kin)], local_sem.at[0]),
        pltpu.make_async_copy(pout, buf.at[f, :, pl.ds(kin, kout)], local_sem.at[1]),
    ]
    loads += [
        pltpu.make_async_copy(hidden.at[:, pl.ds(k * kin, kin)], hid.at[k], local_sem.at[3 + k])
        for k in range(F)
    ]
    loads += [
        pltpu.make_async_copy(out_grad.at[:, pl.ds(k * kout, kout)], ogr.at[k], local_sem.at[3 + F + k])
        for k in range(F)
    ]
    query_load = pltpu.make_async_copy(queries, qry, local_sem.at[2])
    for load in loads[:2]:
        load.start()

    barrier = pltpu.get_barrier_semaphore()
    for dev in ((g, f, d, 1 - s), (g, f, 1 - d, s), (1 - g, f, d, s)):
        pl.semaphore_signal(barrier, inc=1, device_id=dev, device_id_type=MESH)

    @pl.when(f > 0)
    def _():
        pl.semaphore_signal(barrier, inc=1, device_id=(g, f - 1, d, s), device_id_type=MESH)

    @pl.when(f < F - 1)
    def _():
        pl.semaphore_signal(barrier, inc=1, device_id=(g, f + 1, d, s), device_id_type=MESH)

    pl.semaphore_wait(barrier, 3 + jnp.where(f > 0, 1, 0) + jnp.where(f < F - 1, 1, 0))

    mine = g * 2 + d
    col_x, col_y, col_d = g * 2 + (1 - d), (1 - g) * 2 + d, (1 - g) * 2 + (1 - d)
    dev_x, dev_y = (g, f, 1 - d, s), (1 - g, f, d, s)

    def copy(shard, col, part, send, recv, dev):
        rows = pl.ds(pl.multiple_of(col * piece_rows, piece_rows), piece_rows)
        ref = buf.at[shard, rows, pl.ds(part * lanes, lanes)]
        return pltpu.make_async_remote_copy(
            src_ref=ref, dst_ref=ref, send_sem=send, recv_sem=recv,
            device_id=dev, device_id_type=MESH,
        )

    def along_z(shard, k, up):
        dev = (g, f + 1, d, s) if up else (g, f - 1, d, s)
        col, part = (mine, k) if k < PARTS else (col_d, k - THIRD)
        return copy(shard, col, part, zs.at[1 if up else 0, shard, k], zr.at[shard, k], dev)

    def to_x(shard, k):
        col, part = (mine, k) if k < PARTS else (col_y, k - 2 * THIRD)
        return copy(shard, col, part, xs.at[shard, k], xr.at[shard, k], dev_x)

    def to_y(shard, k):
        col, part = (mine, k) if k < PARTS else (col_x, k - PARTS)
        return copy(shard, col, part, ys.at[shard, k], yr.at[shard, k], dev_y)

    def from_x(shard, k):
        col, part = (col_x, k) if k < PARTS else (col_d, k - 2 * THIRD)
        return copy(shard, col, part, xs.at[shard, k], xr.at[shard, k], dev_x)

    def from_y(shard, k):
        col, part = (col_y, k) if k < PARTS else (col_d, k - PARTS)
        return copy(shard, col, part, ys.at[shard, k], yr.at[shard, k], dev_y)

    def project(shard):
        acc[W:, :] += lax.dot_general(
            buf[shard, :, :kin], hid[shard], NT, preferred_element_type=jnp.float32)
        acc[:W, :] += lax.dot_general(
            buf[shard, :, kin:], ogr[shard], NT, preferred_element_type=jnp.float32)

    def each(t, fn, k=None):
        @pl.when(f - t >= 0)
        def _():
            fn(f - t, True, k)

        @pl.when(f + t < F)
        def _():
            fn(f + t, False, k)

    def onward(shard, up, k, act):
        if up:
            @pl.when(f < F - 1)
            def _():
                act(along_z(shard, k, True))
        else:
            @pl.when(f > 0)
            def _():
                act(along_z(shard, k, False))

    loads[0].wait()
    loads[1].wait()
    for k in range(ITEMS):
        for up in (False, True):
            onward(f, up, k, lambda c: c.start())

    for load in loads[2:]:
        load.start()
    query_load.start()
    for load in loads[2:]:
        load.wait()
    acc[...] = jnp.zeros_like(acc)
    project(f)

    def arrive(shard, up, k):
        along_z(shard, k, up).wait_recv()
        onward(shard, up, k, lambda c: c.start())
        if k < PARTS:
            to_x(shard, k).start()
            to_y(shard, k).start()

    def relay(shard, up, k):
        if k < THIRD:
            from_x(shard, k).wait_recv()
            to_y(shard, PARTS + k).start()
        else:
            from_y(shard, k).wait_recv()
            to_x(shard, PARTS + k - THIRD).start()

    def finish(shard, up, k):
        for k in range(THIRD, ITEMS):
            from_x(shard, k).wait_recv()
        for k in [*range(THIRD), *range(2 * THIRD, ITEMS)]:
            from_y(shard, k).wait_recv()
        project(shard)

    items = [(t, k) for t in range(1, F) for k in range(ITEMS)]
    for n in range(len(items) + LAG):
        if n < len(items):
            each(items[n][0], arrive, items[n][1])
        if n >= LAG and items[n - LAG][1] < 2 * THIRD:
            each(items[n - LAG][0], relay, items[n - LAG][1])
        if n < len(items) and items[n][0] > 1 and items[n][1] == ITEMS - 1:
            each(items[n][0] - 1, finish)
    if F > 1:
        each(F - 1, finish)

    p_copy = pltpu.make_async_remote_copy(
        src_ref=acc, dst_ref=part, send_sem=sub_sem.at[0], recv_sem=sub_sem.at[1],
        device_id=(g, f, d, 1 - s), device_id_type=MESH,
    )
    p_copy.start()
    p_copy.wait_recv()
    summed[...] = acc[...] + part[...]

    slot = tokens // 2
    lane = lax.broadcasted_iota(jnp.int32, (W // 2, tokens), 1)
    even = summed[pl.ds(0, W // 2, stride=2), :]
    odd = summed[pl.ds(1, W // 2, stride=2), :]
    first = lane < lengths[0]
    second = jnp.logical_and(lane >= slot, lane < slot + lengths[1])
    left = jnp.concatenate(
        [jnp.where(first, even, 0.0), jnp.where(first, odd, 0.0),
         jnp.where(second, even, 0.0), jnp.where(second, odd, 0.0)], axis=0)
    outer = lax.dot_general(
        left, summed[W:, :], NT, precision=lax.Precision.HIGHEST,
        preferred_element_type=jnp.float32) / math.sqrt(slot)
    hw = W // 2
    pair = f * 2 + d
    own = pl.ds(pair * 2, 2)
    for i in range(2):
        both = jnp.concatenate(
            [outer[2 * i * hw:(2 * i + 1) * hw], outer[(2 * i + 1) * hw:(2 * i + 2) * hw]], axis=1)
        gath[pair * 2 + i] = both.astype(jnp.bfloat16)

    shifts = [(df, dd) for df in range(F) for dd in range(2)][1:]

    def enc_copy(k, owner, dev):
        ref = gath.at[pl.ds(owner * 2, 2)]
        return pltpu.make_async_remote_copy(
            src_ref=ref, dst_ref=ref, send_sem=es.at[k], recv_sem=er.at[owner],
            device_id=dev, device_id_type=MESH)

    def peer(df, dd):
        return lax.rem(f + df, F), lax.rem(d + dd, 2)

    for k, (df, dd) in enumerate(shifts):
        pf, pd = peer(df, dd)
        enc_copy(k, pair, (g, pf, pd, s)).start()
    query_load.wait()
    for k, (df, dd) in enumerate(shifts):
        pf, pd = peer(df, dd)
        enc_copy(k, pf * 2 + pd, (g, pf, pd, s)).wait_recv()

    for e in range(E):
        flat[e * hw:(e + 1) * hw, :] = gath[e].astype(jnp.float32)
    for r in range(hw):
        enc[:, r * 128:(r + 1) * 128] = flat[pl.ds(r, E, stride=hw), :].astype(jnp.bfloat16)

    dims = qry.shape[1]
    score = lax.dot_general(
        enc[:, pl.ds(pl.multiple_of(s * dims, dims), dims)], qry[...], NT,
        preferred_element_type=jnp.float32)
    for p in range(E // 2):
        spart[p] = score[2 * p:2 * p + 2, :]
    targets = [(df, ds) for df in range(F) for ds in range(2)]

    def score_copy(k, src, slot_id, dev):
        return pltpu.make_async_remote_copy(
            src_ref=spart.at[src], dst_ref=sgot.at[slot_id],
            send_sem=ss.at[k], recv_sem=sr.at[slot_id],
            device_id=dev, device_id_type=MESH)

    for k, (df, ds) in enumerate(targets[1:]):
        pf, ps = lax.rem(f + df, F), lax.rem(s + ds, 2)
        score_copy(k, pf * 2 + d, f * 2 + s, (g, pf, d, ps)).start()
    sgot[f * 2 + s] = spart[pair]
    nrow, ncol = rows_out.shape[1], cols_out.shape[1]
    rows_out[...] = enc[:, pl.ds(pl.multiple_of(f * nrow, nrow), nrow)]
    cols_out[...] = enc[:, pl.ds(pl.multiple_of((d * 2 + s) * ncol, ncol), ncol)]
    for k, (df, ds) in enumerate(targets[1:]):
        pf, ps = lax.rem(f + df, F), lax.rem(s + ds, 2)
        score_copy(k, pf * 2 + d, pf * 2 + ps, (g, pf, d, ps)).wait_recv()
    nq = qry.shape[0]
    for k in range(F):
        scores_out[:, k * nq:(k + 1) * nq] = (sgot[2 * k] + sgot[2 * k + 1]) / math.sqrt(2 * dims)

    for k, (df, ds) in enumerate(targets[1:]):
        pf, ps = lax.rem(f + df, F), lax.rem(s + ds, 2)
        score_copy(k, pf * 2 + d, f * 2 + s, (g, pf, d, ps)).wait_send()
    for k, (df, dd) in enumerate(shifts):
        pf, pd = peer(df, dd)
        enc_copy(k, pair, (g, pf, pd, s)).wait_send()
    p_copy.wait_send()

    for k in range(ITEMS):
        for up in (False, True):
            onward(f, up, k, lambda c: c.wait_send())

    def sent(shard, up, k):
        for k in range(ITEMS):
            onward(shard, up, k, lambda c: c.wait_send())
            to_x(shard, k).wait_send()
            to_y(shard, k).wait_send()

    for t in range(1, F):
        each(t, sent)


def fused(F, hidden, out_grad, proj_in, proj_out, queries, lengths):
    examples, slot_len, half_hidden = hidden.shape
    half_model = out_grad.shape[2]
    W = proj_in.shape[2]
    kin, kout = proj_in.shape[1], proj_out.shape[1]
    tokens = examples * slot_len
    nq, dims = queries.shape
    E = F * 2 * examples
    KK = W * W
    hbm = pl.BlockSpec(memory_space=pltpu.HBM)
    vmem = pl.BlockSpec(memory_space=pltpu.VMEM)
    bf, f32 = jnp.bfloat16, jnp.float32
    dma = pltpu.SemaphoreType.DMA
    rows, cols, scores = pl.pallas_call(
        functools.partial(kernel, F),
        out_shape=(
            jax.ShapeDtypeStruct((E, KK // F), bf),
            jax.ShapeDtypeStruct((E, KK // 4), bf),
            jax.ShapeDtypeStruct((examples, nq * F), f32),
        ),
        in_specs=[hbm] * 5 + [pl.BlockSpec(memory_space=pltpu.SMEM)],
        out_specs=(vmem, vmem, vmem),
        scratch_shapes=[
            pltpu.VMEM((F, W, kin + kout), bf),
            pltpu.VMEM((F, tokens, kin), bf),
            pltpu.VMEM((F, tokens, kout), bf),
            pltpu.VMEM((nq, dims), bf),
            pltpu.VMEM((2 * W, tokens), f32),
            pltpu.VMEM((2 * W, tokens), f32),
            pltpu.VMEM((2 * W, tokens), f32),
            pltpu.VMEM((E, W // 2, 2 * W), bf),
            pltpu.VMEM((E * W // 2, 2 * W), f32),
            pltpu.VMEM((E, KK), bf),
            pltpu.VMEM((E // 2, 2, nq), f32),
            pltpu.VMEM((2 * F, 2, nq), f32),
            dma((3 + 2 * F,)),
            dma((2, F, ITEMS)), dma((F, ITEMS)), dma((F, ITEMS)),
            dma((F, ITEMS)), dma((F, ITEMS)), dma((F, ITEMS)),
            dma((2,)),
            dma((2 * F,)), dma((2 * F,)), dma((2 * F,)), dma((2 * F,)),
        ],
        compiler_params=pltpu.CompilerParams(
            collective_id=0, has_side_effects=True, vmem_limit_bytes=60 << 20),
    )(
        hidden.reshape(tokens, half_hidden),
        out_grad.reshape(tokens, half_model),
        jnp.swapaxes(proj_in[0], 0, 1),
        jnp.swapaxes(proj_out[0], 0, 1),
        queries,
        lengths,
    )
    covariance = lax.dot_general(
        rows, cols, (((0,), (0,)), ((), ())), preferred_element_type=f32) / E
    return covariance, scores


def general(hidden, out_grad, proj_in, proj_out, queries, lengths):
    examples, slot_len, half_hidden = hidden.shape
    half_model = out_grad.shape[2]
    W = proj_in.shape[2]
    tokens = examples * slot_len
    f32 = jnp.float32
    inputs_part = jnp.dot(
        hidden.reshape(tokens, half_hidden),
        lax.all_gather(proj_in, "fsdp", axis=1, tiled=True)[0],
        preferred_element_type=f32)
    grads_part = jnp.dot(
        out_grad.reshape(tokens, half_model),
        lax.all_gather(proj_out, "fsdp", axis=1, tiled=True)[0],
        preferred_element_type=f32)
    summed = lax.psum(jnp.concatenate((grads_part, inputs_part), axis=1), "sub")
    low_grads = summed[:, :W].reshape(examples, slot_len, W)
    low_inputs = summed[:, W:].reshape(examples, slot_len, W)
    live = (jnp.arange(slot_len, dtype=jnp.int32)[None, :] < lengths[:, None]).astype(f32)
    encoded = jnp.einsum(
        "eta,etb->eab", low_grads * live[:, :, None], low_inputs,
        precision=lax.Precision.HIGHEST) / math.sqrt(slot_len)
    KK = W * W
    encoded = encoded.reshape(examples, KK).astype(jnp.bfloat16)
    F, Dp, S = lax.axis_size("fsdp"), lax.axis_size("dp"), lax.axis_size("sub")
    everyone = lax.all_gather(encoded, ("fsdp", "dp"), axis=0, tiled=True)
    nrow, ncol, half = KK // F, KK // (Dp * S), KK // S
    rows = lax.dynamic_slice_in_dim(everyone, lax.axis_index("fsdp") * nrow, nrow, 1)
    cols = lax.dynamic_slice_in_dim(
        everyone, (lax.axis_index("dp") * S + lax.axis_index("sub")) * ncol, ncol, 1)
    covariance = lax.dot_general(
        rows, cols, (((0,), (0,)), ((), ())), preferred_element_type=f32) / everyone.shape[0]
    own_half = lax.dynamic_slice_in_dim(encoded, lax.axis_index("sub") * half, half, 1)
    partial_scores = lax.dot_general(
        own_half, lax.all_gather(queries, "fsdp", axis=0, tiled=True),
        (((1,), (1,)), ((), ())), preferred_element_type=f32)
    scores = lax.psum(partial_scores, "sub") / math.sqrt(KK)
    return covariance, scores


def solution(mesh):
    sizes = dict(mesh.shape)
    placed = (
        P(("groups", "fsdp", "dp"), None, "sub"),
        P(("groups", "fsdp", "dp"), None, "sub"),
        P("sub", "fsdp", None),
        P("sub", "fsdp", None),
        P("fsdp", "sub"),
        P(("groups", "fsdp", "dp")),
    )
    square = sizes["groups"] == 2 and sizes["dp"] == 2 and sizes["fsdp"] <= 4
    body = functools.partial(fused, sizes["fsdp"]) if square else general
    return jax.shard_map(
        body,
        mesh=mesh,
        in_specs=placed,
        out_specs=(P(("groups", "fsdp"), ("dp", "sub")), P(("groups", "fsdp", "dp"), None)),
        check_vma=False,
    )
```
